256 devices in a mesh: dp: 32 (over z, y_lo, core), seq: 8 (over y_hi, x).
Axes of the slice: x: 4, y: 4 (y_hi: 2, y_lo: 2; y = y_hi * 2 + y_lo), z: 8, core: 2. Of those that a mesh axis runs over, the one named last changes fastest.
Arguments:
- resp_q: bfloat16 [32, 8, 256, 2048], P('dp', 'seq'), may hold values from -32 to 32
- resp_k: bfloat16 [32, 8, 256, 2048], P('dp', 'seq'), may hold values from -4 to 4
- resp_v: bfloat16 [32, 8, 256, 2048], P('dp', 'seq'), may hold values from -6 to 6
- resp_grad: bfloat16 [32, 8, 256, 2048], P('dp', 'seq'), may hold values from -192 to 192
- prompt_k: bfloat16 [32, 8, 64, 2048], P('dp', 'seq'), may hold values from -6 to 6
- prompt_v: bfloat16 [32, 8, 64, 2048], P('dp', 'seq'), may hold values from -6 to 6
- group: int32 [32], replicated, may hold values from 0 to 31, each once
- resp_len: int32 [32, 8], P('dp', 'seq'), may hold values from 128 to 256, as said below
- prompt_used: int32 [32], replicated, may hold values from 256 to 512, as said below
Outputs:
- grad_q: bfloat16 [32, 8, 256, 2048], P('dp', 'seq')
- grad_k: bfloat16 [32, 8, 256, 2048], P('dp', 'seq')
- grad_v: bfloat16 [32, 8, 256, 2048], P('dp', 'seq')
- grad_prompt_k: bfloat16 [32, 8, 64, 2048], P('dp', 'seq')
- grad_prompt_v: bfloat16 [32, 8, 64, 2048], P('dp', 'seq')
The draws below stay inside these ranges and needn't reach their ends.
Inputs may be any that keep to these rules, and one draw needn't show every extreme that they name: group is a permutation: every prompt is named by exactly one response group. `resp_len`: multiples of 128; the largest equals 256. `prompt_used`: multiples of 64, at least half of 512; the largest equals 512.
All inputs are finite; a program needn't handle non-finite values.
Results may differ from the reference program's by a relative error of at most 0.017.
Values may be sent and summed in bfloat16 or wider, within the bound.
A program may use at most 128 MiB of HBM per device.

```python
import jax
import jax.numpy as jnp
from jax import lax

HEADS = 16
HEAD_DIM = 128
BLOCK = 128
RB = 2
PL_DEV = 64
RL = 256
HD = 2048
N_DP = 32
N_SEQ = 8


def aligned_parts(key):
    groups = RB * BLOCK // 8
    shape = (N_DP, N_SEQ, groups, HEADS * HEAD_DIM)
    signs = jnp.where(jax.random.bernoulli(jax.random.fold_in(key, 101), 0.5, shape), 1.0, -1.0)
    return jnp.repeat(signs, 8, axis=2)


def draw_resp_q(key, part):
    signs = aligned_parts(key)
    key = jax.random.fold_in(key, 1)
    entries = jnp.clip(jax.random.normal(key, signs.shape, jnp.float32), -6.0, 6.0)
    values = entries
    return values.astype(jnp.bfloat16)


def draw_resp_k(key, part):
    signs = aligned_parts(key)
    key = jax.random.fold_in(key, 2)
    values = jnp.clip(jax.random.normal(key, signs.shape, jnp.float32), -4.0, 4.0)
    return values.astype(jnp.bfloat16)


def draw_resp_len(key, part):
    key = jax.random.fold_in(key, 5)
    drawn = jax.random.randint(key, (N_DP, N_SEQ), 1, RB + 1) * BLOCK
    return drawn.at[0, 0].set(RB * BLOCK).astype(jnp.int32)


def draw_prompt_used(key, part):
    key = jax.random.fold_in(key, 7)
    lowest = N_SEQ // 2
    highest = N_SEQ
    drawn = jax.random.randint(key, (N_DP,), lowest, highest + 1) * PL_DEV
    return drawn.at[0].set(highest * PL_DEV).astype(jnp.int32)


def levels(key, shape, pieces, least, top_value):
    def one(dim, blocks):
        heights = jax.random.uniform(jax.random.fold_in(jax.random.fold_in(key, 6), dim), (blocks,), jnp.float32, least / len(pieces), top_value / len(pieces))
        return jnp.repeat(jnp.exp(heights), shape[dim] // blocks).reshape((-1,) + (1,) * (len(shape) - dim - 1))

    level = one(*pieces[0])
    for cut in pieces[1:]:
        level = level * one(*cut)
    return level


def normal_values(own_key, dims, scale, reach, cuts=(), kind=jnp.bfloat16):
    gain = levels(own_key, dims, cuts, -0.22, 0.18) if cuts else 1.0
    values = jax.random.normal(own_key, dims, jnp.float32) * scale * gain
    return jnp.minimum(jnp.maximum(values, -reach), reach).astype(kind)


def setup_inputs(seed: int = 0) -> dict:
    streams_of = jax.random.split(jax.random.key(seed), 10)
    resp_q = draw_resp_q(jax.random.fold_in(streams_of[9], 71), 0)
    resp_k = draw_resp_k(jax.random.fold_in(streams_of[9], 71), 0)
    resp_v = normal_values(streams_of[2], (N_DP, N_SEQ, RL, HD), 1.0, 6.0, ((0, 32), (1, 8)))
    resp_grad = normal_values(streams_of[3], (N_DP, N_SEQ, RL, HD), 32.0, 192.0, ((0, 32), (1, 8)))
    prompt_k = normal_values(streams_of[4], (N_DP, N_SEQ, PL_DEV, HD), 1.0, 6.0, ((0, 32), (1, 8)))
    prompt_v = normal_values(streams_of[5], (N_DP, N_SEQ, PL_DEV, HD), 1.0, 6.0, ((0, 32), (1, 8)))
    group = jax.random.permutation(streams_of[6], N_DP).astype(jnp.int32)
    resp_len = draw_resp_len(jax.random.fold_in(streams_of[9], 71), 0)
    prompt_used = draw_prompt_used(jax.random.fold_in(streams_of[9], 71), 0)
    return {"resp_q": resp_q, "resp_k": resp_k, "resp_v": resp_v, "resp_grad": resp_grad, "prompt_k": prompt_k, "prompt_v": prompt_v, "group": group, "resp_len": resp_len, "prompt_used": prompt_used}


NEG = -1.0e30


def one_response(query, key_own, value_own, grad_out, key_prompt, value_prompt, used, length):
    rows = query.shape[0]
    plen = key_prompt.shape[0]
    width = query.shape[1]
    scale = HEAD_DIM ** -0.5
    queries = query.reshape(rows, HEADS, HEAD_DIM).astype(jnp.float32)
    keys = jnp.concatenate([key_prompt, key_own], axis=0).reshape(plen + rows, HEADS, HEAD_DIM).astype(jnp.float32)
    values = jnp.concatenate([value_prompt, value_own], axis=0).reshape(plen + rows, HEADS, HEAD_DIM).astype(jnp.float32)
    positions = jnp.arange(rows, dtype=jnp.int32)
    masked = jnp.where((positions < length)[:, None], grad_out, jnp.zeros_like(grad_out))
    masked = masked.reshape(rows, HEADS, HEAD_DIM).astype(jnp.float32)
    key_pos = jnp.arange(plen + rows, dtype=jnp.int32) - plen
    prompt_ok = (key_pos + plen) < used
    own_ok = (key_pos[None, :] <= positions[:, None]) & (key_pos[None, :] < length)
    valid = jnp.where((key_pos < 0)[None, :], prompt_ok[None, :], own_ok)
    scores = jnp.einsum('ihd,jhd->hij', queries, keys) * scale
    scores = jnp.where(valid[None], scores, NEG)
    top = jnp.max(scores, axis=-1)
    total = jnp.sum(jnp.where(valid[None], jnp.exp(scores - top[..., None]), 0.0), axis=-1)
    lse = top + jnp.log(total)
    probs = jnp.where(valid[None], jnp.exp(scores - lse[..., None]), 0.0)
    dots = jnp.einsum('ihd,jhd->hij', masked, values)
    delta = jnp.sum(probs * dots, axis=-1)
    probs_low = lax.optimization_barrier(probs.astype(jnp.bfloat16)).astype(jnp.float32)
    slopes = lax.optimization_barrier((probs * (dots - delta[..., None])).astype(jnp.bfloat16)).astype(jnp.float32)
    grad_values = jnp.einsum('hij,ihd->jhd', probs_low, masked).reshape(plen + rows, width)
    grad_keys = (jnp.einsum('hij,ihd->jhd', slopes, queries) * scale).reshape(plen + rows, width)
    grad_query = (jnp.einsum('hij,jhd->ihd', slopes, keys) * scale).reshape(rows, width)
    return (grad_query.astype(jnp.bfloat16), grad_keys[plen:].astype(jnp.bfloat16),
            grad_values[plen:].astype(jnp.bfloat16), grad_keys[:plen].astype(jnp.bfloat16),
            grad_values[:plen].astype(jnp.bfloat16))


def reference(resp_q, resp_k, resp_v, resp_grad, prompt_k, prompt_v, group, resp_len, prompt_used):
    count = prompt_k.shape[0]
    width = prompt_k.shape[-1]
    keys_all = prompt_k.reshape(count, -1, width)
    values_all = prompt_v.reshape(count, -1, width)
    shards = resp_q.shape[1]

    def per_row(row):
        chosen = group[row].astype(jnp.int32)
        key_prompt = keys_all[chosen]
        value_prompt = values_all[chosen]
        used = prompt_used[chosen]

        def per_seq(column):
            return one_response(resp_q[row, column], resp_k[row, column], resp_v[row, column],
                                resp_grad[row, column], key_prompt, value_prompt, used, resp_len[row, column])

        grad_query, grad_keys, grad_values, part_k, part_v = lax.map(per_seq, jnp.arange(shards, dtype=jnp.int32))
        sum_k = jnp.sum(part_k.astype(jnp.float32), axis=0).astype(jnp.bfloat16)
        sum_v = jnp.sum(part_v.astype(jnp.float32), axis=0).astype(jnp.bfloat16)
        return grad_query, grad_keys, grad_values, sum_k, sum_v

    grad_q, grad_k, grad_v, rows_k, rows_v = lax.map(per_row, jnp.arange(count, dtype=jnp.int32))
    grad_prompt_k = jnp.zeros_like(keys_all).at[group].add(rows_k).reshape(prompt_k.shape)
    grad_prompt_v = jnp.zeros_like(values_all).at[group].add(rows_v).reshape(prompt_v.shape)
    return grad_q, grad_k, grad_v, grad_prompt_k, grad_prompt_v
```

```python
import functools

import jax
import jax.numpy as jnp
from jax import lax
from jax.experimental import pallas as pl
from jax.experimental.pallas import tpu as pltpu
from jax.sharding import PartitionSpec as P

HEADS = 16
NEG = -1e30
LOG2E = 1.4426950408889634
NT = (((1,), (1,)), ((), ()))
TN = (((0,), (0,)), ((), ()))
NN = (((1,), (0,)), ((), ()))


def dot(a, b, dims):
    return lax.dot_general(a, b, dims, preferred_element_type=jnp.float32)


def head_grads(q, g, kp, ko, vp, vo, bias_p, bias_o, scale):
    c = scale * LOG2E
    sp = dot(kp, q, NT) * c + bias_p
    so = dot(ko, q, NT) * c + bias_o
    top = jnp.maximum(jnp.max(sp, 0, keepdims=True), jnp.max(so, 0, keepdims=True))
    pp = jnp.exp2(sp - top)
    po = jnp.exp2(so - top)
    inv = 1.0 / (jnp.sum(pp, 0, keepdims=True) + jnp.sum(po, 0, keepdims=True))
    dp = dot(vp, g, NT)
    do = dot(vo, g, NT)
    delta = (jnp.sum(pp * dp, 0, keepdims=True) + jnp.sum(po * do, 0, keepdims=True)) * inv
    pp = pp * inv
    po = po * inv
    lp = pp.astype(jnp.bfloat16)
    lo = po.astype(jnp.bfloat16)
    tp = (pp * (dp - delta)).astype(jnp.bfloat16)
    to = (po * (do - delta)).astype(jnp.bfloat16)
    gq = (dot(tp, kp, TN) + dot(to, ko, TN)) * scale
    gko = dot(to, q, NN) * scale
    gvo = dot(lo, g, NN)
    gkp = dot(tp, q, NN) * scale
    gvp = dot(lp, g, NN)
    return tuple(x.astype(jnp.bfloat16) for x in (gq, gko, gvo, gkp, gvp))


def grads_kernel(step, scale, used, length, q, k, v, g, kp, vp, gq, gk, gv, pk, pv):
    rows, plen = q.shape[0], kp.shape[0]
    bias_p = jnp.where(lax.broadcasted_iota(jnp.int32, (plen, rows), 0) < used[0], 0.0, NEG)
    key = lax.broadcasted_iota(jnp.int32, (rows, rows), 0)
    query = lax.broadcasted_iota(jnp.int32, (rows, rows), 1)
    bias_o = jnp.where((key <= query) & (key < length[0]), 0.0, NEG)
    live = lax.broadcasted_iota(jnp.int32, (rows, 128), 0) < length[0]
    for u in range(step):
        s = slice(u * 128, u * 128 + 128)
        masked = jnp.where(live, g[:, s], jnp.zeros_like(g[:, s]))
        gq[:, s], gk[:, s], gv[:, s], pk[:, s], pv[:, s] = head_grads(
            q[:, s], masked, kp[:, s], k[:, s], vp[:, s], v[:, s], bias_p, bias_o, scale
        )


def grads(q, k, v, g, kp, vp, used, length):
    rows, width = q.shape
    plen = kp.shape[0]
    step = 2
    own = pl.BlockSpec((rows, 128 * step), lambda h: (0, h))
    prompt = pl.BlockSpec((plen, 128 * step), lambda h: (0, h))
    scalar = pl.BlockSpec(memory_space=pltpu.SMEM)
    shape = lambda r: jax.ShapeDtypeStruct((r, width), jnp.bfloat16)
    return pl.pallas_call(
        functools.partial(grads_kernel, step, 128**-0.5),
        grid=(width // (128 * step),),
        in_specs=[scalar, scalar, own, own, own, own, prompt, prompt],
        out_specs=[own, own, own, prompt, prompt],
        out_shape=[shape(rows)] * 3 + [shape(plen)] * 2,
        compiler_params=pltpu.CompilerParams(vmem_limit_bytes=40 * 2**20),
    )(used, length, q, k, v, g, kp, vp)


def on_device(resp_q, resp_k, resp_v, resp_grad, prompt_k, prompt_v, group, resp_len, prompt_used):
    rows, width = resp_q.shape[2:]
    count = lax.axis_size("dp")
    mine = lax.axis_index("dp")
    slots = jnp.arange(count, dtype=jnp.int32)
    chosen = jnp.sum(jnp.where(slots == mine, group, 0))
    used = jnp.sum(jnp.where(slots == chosen, prompt_used, 0))
    shard_rows = prompt_k.shape[2]
    piece_rows = shard_rows // count
    stacked = jnp.stack([prompt_k[0, 0], prompt_v[0, 0]], axis=0).reshape(
        2, count, piece_rows, width
    )
    spread_out = lax.all_to_all(stacked, "dp", split_axis=1, concat_axis=1, tiled=True)
    outgoing = jnp.take(spread_out, group, axis=1)
    arrived = lax.all_to_all(outgoing, "dp", split_axis=1, concat_axis=1, tiled=True)
    shard = arrived.reshape(2, shard_rows, width)
    whole = lax.all_gather(shard, "seq", axis=1, tiled=True)
    grad_q, grad_k, grad_v, part_k, part_v = grads(
        resp_q[0, 0], resp_k[0, 0], resp_v[0, 0], resp_grad[0, 0],
        whole[0], whole[1], used.reshape(1), resp_len[0],
    )
    buffer = jnp.stack([part_k, part_v], axis=0)
    summed = lax.psum_scatter(buffer, "seq", scatter_dimension=1, tiled=True)
    returned = summed.reshape(2, count, piece_rows, width)
    back = lax.all_to_all(returned, "dp", split_axis=1, concat_axis=1, tiled=True)
    owner_table = group[None, :] == slots[:, None]
    inverse = jnp.sum(jnp.where(owner_table, slots[None, :], 0), axis=1)
    ordered = jnp.take(back, inverse, axis=1)
    owned = lax.all_to_all(ordered, "dp", split_axis=1, concat_axis=1, tiled=True).reshape(
        2, shard_rows, width
    )
    return (
        grad_q[None, None], grad_k[None, None], grad_v[None, None],
        owned[0][None, None], owned[1][None, None],
    )


def solution(mesh):
    split = P("dp", "seq", None, None)
    return jax.shard_map(
        on_device,
        mesh=mesh,
        in_specs=(split,) * 6 + (P(), P("dp", "seq"), P()),
        out_specs=(split,) * 5,
        check_vma=False,
    )
```

```python
import functools

import jax
import jax.numpy as jnp
from jax import lax
from jax.experimental import pallas as pl
from jax.experimental.pallas import tpu as pltpu
from jax.sharding import PartitionSpec as P

HEAD = 128
TILE = 16
CHUNKS = 4
NX = 4
NEG = -1e30
LOG2E = 1.4426950408889634
NT = (((1,), (1,)), ((), ()))
TN = (((0,), (0,)), ((), ()))
NN = (((1,), (0,)), ((), ()))
MESH = pl.DeviceIdType.MESH
BF16 = jnp.bfloat16
F32 = jnp.float32

GATHER_Y_FIRST = ((True, False), (True, False), (True, True), (True, True))
SCATTER_Y_LAST = ((True, False), (True, False), (True, True), (True, True))


PLAN = (
    ("p1", 3), ("p1", 0), ("prep",), ("p2", 3), ("p2", 0), ("p1", 1), ("p1", 2), ("a0", 3), ("au", 3, 0),
    ("ad", 3, 0), ("a0", 0), ("as", 3, 0), ("p2", 1), ("as", 3, 1), ("au", 0, 1), ("ad", 0, 1), ("as", 0, 0),
    ("p2", 2), ("ad", 0, 0), ("au", 0, 0), ("aou", 3, 0), ("aod", 3, 1), ("aou", 3, 1), ("ad", 3, 1), ("au", 3, 1),
    ("af", 0, 1), ("aod", 3, 0), ("aou", 0, 0), ("aod", 0, 0), ("a0", 1), ("a0", 2), ("a3", 3), ("k", 3, 0),
    ("a3", 0), ("k", 0, 0), ("k", 0, 1), ("ad", 1, 0), ("ad", 1, 1), ("as", 2, 0), ("k", 0, 2), ("au", 1, 1),
    ("k", 0, 3), ("as", 1, 0), ("r0", 0, 0), ("as", 2, 1), ("r0", 0, 1), ("au", 2, 0), ("k", 3, 1), ("k", 3, 2),
    ("aod", 1, 0), ("aou", 1, 0), ("au", 1, 0), ("k", 3, 3), ("r0", 3, 0), ("r0", 3, 1), ("aod", 2, 0),
    ("rn", 0, 0, 1, 0), ("rn", 0, 0, 0, 0), ("rn", 0, 0, 1, 1), ("aou", 2, 0), ("af", 1, 1), ("ad", 2, 1),
    ("rr", 0, 1), ("a3", 1), ("k", 1, 0), ("au", 2, 1), ("ad", 2, 0), ("rn", 3, 1, 1, 1), ("k", 1, 1), ("k", 1, 2),
    ("rt", 0, 0), ("k", 1, 3), ("r0", 1, 1), ("aou", 2, 1), ("aod", 2, 1), ("rn", 3, 0, 1, 0), ("rn", 3, 0, 1, 1),
    ("rn", 0, 1, 0, 0), ("rn", 3, 1, 1, 0), ("rn", 3, 0, 0, 0), ("rn", 0, 0, 0, 1), ("rn", 3, 1, 0, 0),
    ("rn", 0, 1, 0, 1), ("rn", 3, 0, 0, 1), ("a3", 2), ("k", 2, 0), ("k", 2, 1), ("k", 2, 2), ("rn", 3, 1, 0, 1),
    ("rt", 3, 0), ("k", 2, 3), ("r0", 2, 1), ("rt", 3, 1), ("r0", 2, 0), ("rf", 0, 1), ("rf", 0, 0), ("p3", 0),
    ("rr", 1, 1), ("rn", 2, 1, 1, 0), ("rf", 3, 0), ("r0", 1, 0), ("rf", 3, 1), ("rn", 2, 1, 1, 1), ("p3", 3),
    ("rn", 2, 0, 1, 0), ("rn", 2, 0, 0, 0), ("rn", 2, 0, 1, 1), ("rn", 1, 0, 1, 1), ("p4", 0), ("rn", 2, 0, 0, 1),
    ("rn", 2, 1, 0, 1), ("rt", 2, 1), ("rn", 1, 0, 1, 0), ("rn", 2, 1, 0, 0), ("rn", 1, 0, 0, 1),
    ("rn", 1, 0, 0, 0), ("rt", 2, 0), ("p4", 3), ("rt", 1, 0), ("rn", 1, 1, 0, 1), ("rn", 1, 1, 0, 0), ("rf", 2, 0),
    ("rf", 2, 1), ("p3", 2), ("rf", 1, 1), ("rf", 1, 0), ("p3", 1), ("p4", 2), ("p4", 1), ("end", 2), ("end", 3),
    ("end", 0), ("end", 1),
)


def dot(a, b, dims):
    return lax.dot_general(a, b, dims, preferred_element_type=F32)


def head_grads(q, g, kp, ko, vp, vo, bias_p, bias_o, scale):
    c = scale * LOG2E
    sp = dot(kp, q, NT) * c + bias_p
    so = dot(ko, q, NT) * c + bias_o
    top = jnp.maximum(jnp.max(sp, 0, keepdims=True), jnp.max(so, 0, keepdims=True))
    pp = jnp.exp2(sp - top)
    po = jnp.exp2(so - top)
    inv = 1.0 / (jnp.sum(pp, 0, keepdims=True) + jnp.sum(po, 0, keepdims=True))
    dp = dot(vp, g, NT)
    do = dot(vo, g, NT)
    delta = (jnp.sum(pp * dp, 0, keepdims=True) + jnp.sum(po * do, 0, keepdims=True)) * inv
    pp = pp * inv
    po = po * inv
    lp = pp.astype(BF16)
    lo = po.astype(BF16)
    tp = (pp * (dp - delta)).astype(BF16)
    to = (po * (do - delta)).astype(BF16)
    gq = (dot(tp, kp, TN) + dot(to, ko, TN)) * scale
    gko = dot(to, q, NN) * scale
    gvo = dot(lo, g, NN)
    gkp = dot(tp, q, NN) * scale
    gvp = dot(lp, g, NN)
    return tuple(x.astype(BF16) for x in (gq, gko, gvo, gkp, gvp))


class Copies:
    def __init__(self, send, recv):
        self.send, self.recv, self.held = send, recv, {}

    def start(self, name, src, dst, target):
        i = len(self.held)
        copy = pltpu.make_async_remote_copy(
            src_ref=src, dst_ref=dst, send_sem=self.send.at[i], recv_sem=self.recv.at[i],
            device_id=target, device_id_type=MESH,
        )
        copy.start()
        self.held[name] = copy

    def arrived(self, name):
        self.held[name].wait_recv()

    def finish(self):
        for copy in self.held.values():
            copy.wait_send()


def kernel(
    count, heads,
    q_in, k_in, v_in, g_in, pk_in, pv_in, group, used_in, len_in,
    gq_out, gk_out, gv_out, pk_out, pv_out,
    q, k, v, g, gq, gk, gv, pin, pout, chosen, gat, part, half_in, full_in, row_in, side_in,
    fin, ordered, bias, inverse,
    load_sem, store_sem, dp_send, dp_recv, seq_send, seq_recv, *held,
):
    stage, back = held[:CHUNKS], held[CHUNKS:]
    rows = q.shape[0]
    shard = pin.shape[1]
    plen = gat.shape[3]
    scale = HEAD**-0.5
    blocks = shard // TILE
    dp = lax.axis_index("dp")
    seq = lax.axis_index("seq")
    yh, x = seq // NX, seq % NX
    x_up, x_down, x_far = (x + 1) % NX, (x + NX - 1) % NX, (x + 2) % NX
    up = (dp, yh * NX + x_up)
    down = (dp, yh * NX + x_down)
    side = (dp, (1 - yh) * NX + x)
    copies = Copies(seq_send, seq_recv)

    def shard_rows(y, xx):
        return pl.ds(pl.multiple_of((y * NX + xx) * shard, shard), shard)

    def place(j):
        return j // (heads * blocks), (j // blocks) % heads, pl.multiple_of((j % blocks) * TILE, TILE)

    def in_shard(ref, c, j):
        kv, h, r = place(j)
        cols = pl.multiple_of((c * heads + h) * HEAD, HEAD)
        return ref.at[kv, pl.ds(r, TILE), pl.ds(cols, HEAD)]

    def spread(phase, c, src, dst):
        def one(k, carry):
            j = (dp + count // 2 + (1 - 2 * (k % 2)) * ((k + 1) // 2)) % count
            pltpu.make_async_remote_copy(
                src_ref=src(j), dst_ref=dst, send_sem=dp_send.at[phase, c],
                recv_sem=dp_recv.at[phase, c], device_id=(j, seq), device_id_type=MESH,
            ).start()
            return carry

        begun.append((phase, c))
        lax.fori_loop(0, count - 1, one, 0)

    begun = []

    def all_of(phase, c, sems):
        some = chosen.at[c, pl.ds(0, count - 1)]
        pltpu.make_async_copy(some, some, sems.at[phase, c]).wait()

    mine = place(dp)

    def p1(c):
        spread(0, c, lambda j: in_shard(pin, c, j), stage[c].at[dp])

    def p2(c):
        stage[c][dp] = in_shard(pin, c, dp)[...]
        all_of(0, c, dp_recv)

        def pick(b, carry):
            chosen[c, b] = stage[c][group[b]]
            return carry

        lax.fori_loop(0, count, pick, 0)
        kv, h, r = mine
        dst = gat.at[c, kv, h, pl.ds(pl.multiple_of(seq * shard + r, TILE), TILE)]
        spread(1, c, lambda j: chosen.at[c, j], dst)
        dst[...] = chosen[c, dp]

    def a0(c):
        all_of(1, c, dp_recv)
        for u in (0, 1):
            own = gat.at[c, u, :, shard_rows(yh, x)]
            for name, to in (("side", side), ("up", up), ("down", down)):
                copies.start(("a", c, u, name), own, own, to)

    def relay_up(c, u, name, y):
        piece = gat.at[c, u, pl.ds(0, heads // 2), shard_rows(y, x_down)]
        copies.start(("a", c, u, name), piece, piece, up)

    def relay_down(c, u, name, y):
        piece = gat.at[c, u, pl.ds(heads // 2, heads // 2), shard_rows(y, x_up)]
        copies.start(("a", c, u, name), piece, piece, down)

    def to_side(c, u, name, xx):
        piece = gat.at[c, u, :, shard_rows(yh, xx)]
        copies.start(("a", c, u, name), piece, piece, side)

    def au(c, u):
        copies.arrived(("a", c, u, "up"))
        relay_up(c, u, "up2", yh)
        if not GATHER_Y_FIRST[c][u]:
            to_side(c, u, "sup", x_down)

    def ad(c, u):
        copies.arrived(("a", c, u, "down"))
        relay_down(c, u, "down2", yh)
        if not GATHER_Y_FIRST[c][u]:
            to_side(c, u, "sdn", x_up)

    def across(c, u):
        copies.arrived(("a", c, u, "side"))
        other = gat.at[c, u, :, shard_rows(1 - yh, x)]
        copies.start(("a", c, u, "oup"), other, other, up)
        copies.start(("a", c, u, "odn"), other, other, down)

    def aou(c, u):
        copies.arrived(("a", c, u, "oup"))
        relay_up(c, u, "oup2", 1 - yh)

    def aod(c, u):
        copies.arrived(("a", c, u, "odn"))
        relay_down(c, u, "odn2", 1 - yh)

    def af(c, u):
        copies.arrived(("a", c, u, "up2"))
        copies.arrived(("a", c, u, "down2"))
        to_side(c, u, "sfar", x_far)

    def a3(c):
        for u in (0, 1):
            if GATHER_Y_FIRST[c][u]:
                names = ("up2", "down2", "oup2", "odn2")
            else:
                names = ("side", "sup", "sdn", "sfar")
            for name in names:
                copies.arrived(("a", c, u, name))

    def compute(c, h):
        cols = pl.ds((c * heads + h) * HEAD, HEAD)
        gq[:, cols], gk[:, cols], gv[:, cols], part[c, 0, h], part[c, 1, h] = head_grads(
            q[:, cols], g[:, cols], gat[c, 0, h], k[:, cols], gat[c, 1, h], v[:, cols],
            bias[:plen], bias[plen:], scale,
        )
        if h == heads - 1:
            store(c)

    def add(dst, src):
        dst[...] = (dst[...].astype(F32) + src[...].astype(F32)).astype(BF16)

    def far_halves(c, u, r, y):
        for d, lo, to in ((0, 0, down), (1, heads // 2, up)):
            copies.start(
                ("r", c, u, r, "half", d),
                part.at[c, u, pl.ds(lo, heads // 2), shard_rows(y, x_far)], half_in.at[c, u, r, d], to,
            )

    def row_of(r):
        return yh if r == 0 else 1 - yh

    def r0(c, u):
        if SCATTER_Y_LAST[c][u]:
            for r in (1, 0):
                far_halves(c, u, r, row_of(r))
        else:
            src = part.at[c, u, :, pl.ds(pl.multiple_of((1 - yh) * NX * shard, shard), NX * shard)]
            copies.start(("r", c, u, "row"), src, row_in.at[c, u], side)

    def rr(c, u):
        copies.arrived(("r", c, u, "row"))
        for xx in (x_far, x_down, x_up, x):
            src = row_in.at[c, u, :, pl.ds(pl.multiple_of(xx * shard, shard), shard)]
            add(part.at[c, u, :, shard_rows(yh, xx)], src)
            if xx is x_far:
                far_halves(c, u, 0, yh)

    def rn(c, u, r, d):
        lo, xx, to = ((0, x_down, down), (heads // 2, x_up, up))[d]
        copies.arrived(("r", c, u, r, "half", d))
        add(part.at[c, u, pl.ds(lo, heads // 2), shard_rows(row_of(r), xx)], half_in.at[c, u, r, d])
        src = part.at[c, u, :, shard_rows(row_of(r), xx)]
        copies.start(("r", c, u, r, "full", d), src, full_in.at[c, u, r, d], to)

    def total(c, u, r):
        for d in (0, 1):
            copies.arrived(("r", c, u, r, "full", d))
        own = part[c, u, :, shard_rows(row_of(r), x)].astype(F32)
        return own + full_in[c, u, r, 0].astype(F32) + full_in[c, u, r, 1].astype(F32)

    def rt(c, u):
        sent = part.at[c, u, :, shard_rows(1 - yh, x)]
        sent[...] = total(c, u, 1).astype(BF16)
        copies.start(("r", c, u, "side"), sent, side_in.at[c, u], side)

    def rf(c, u):
        value = total(c, u, 0)
        if SCATTER_Y_LAST[c][u]:
            copies.arrived(("r", c, u, "side"))
            value = value + side_in[c, u].astype(F32)
        n = heads * blocks
        fin[c, u * n : (u + 1) * n] = value.astype(BF16).reshape(n, TILE, HEAD)

    def p3(c):
        back[c][dp] = fin[c, dp]
        spread(2, c, lambda j: fin.at[c, j], back[c].at[dp])

    def p4(c):
        all_of(2, c, dp_recv)

        def pick(p, carry):
            ordered[c, p] = back[c][inverse[p]]
            return carry

        lax.fori_loop(0, count, pick, 0)
        dst = in_shard(pout, c, dp)
        dst[...] = ordered[c, dp]
        spread(3, c, lambda j: ordered.at[c, j], dst)

    loads = [
        pltpu.make_async_copy(a, b, load_sem.at[i])
        for i, (a, b) in enumerate(
            ((pk_in, pin.at[0]), (pv_in, pin.at[1]), (q_in, q), (k_in, k), (v_in, v), (g_in, g))
        )
    ]
    for copy in loads:
        copy.start()
    barrier = pltpu.get_barrier_semaphore()

    def greet(i, carry):
        pl.semaphore_signal(barrier, inc=1, device_id=((dp + i) % count, seq), device_id_type=MESH)
        return carry

    lax.fori_loop(1, count, greet, 0)
    for target in (up, down, side):
        pl.semaphore_signal(barrier, inc=1, device_id=target, device_id_type=MESH)
    pl.semaphore_wait(barrier, count - 1 + 3)
    loads[0].wait()
    loads[1].wait()

    def prepare():
        length = len_in[0]
        used = used_in[group[dp]]
        bias[:plen] = jnp.where(lax.broadcasted_iota(jnp.int32, (plen, rows), 0) < used, 0.0, NEG)
        key = lax.broadcasted_iota(jnp.int32, (rows, rows), 0)
        query = lax.broadcasted_iota(jnp.int32, (rows, rows), 1)
        bias[plen:] = jnp.where((key <= query) & (key < length), 0.0, NEG)

        def invert(p, carry):
            found = jnp.int32(0)
            for b in range(count):
                found = jnp.where(group[b] == p, b, found)
            inverse[p] = found
            return carry

        lax.fori_loop(0, count, invert, 0)
        for copy in loads[2:]:
            copy.wait()
        for i in range(0, g.shape[1], 512):
            live = lax.broadcasted_iota(jnp.int32, (rows, 512), 0) < length
            g[:, i : i + 512] = jnp.where(live, g[:, i : i + 512], jnp.zeros((rows, 512), BF16))

    stores = []

    def end(c):
        all_of(3, c, dp_recv)

    def store(c):
        cols = pl.ds(c * heads * HEAD, heads * HEAD)
        for i, (a, b) in enumerate(((gq, gq_out), (gk, gk_out), (gv, gv_out))):
            copy = pltpu.make_async_copy(a.at[:, cols], b.at[:, cols], store_sem.at[c, i])
            copy.start()
            stores.append(copy)

    steps = {
        "prep": prepare, "p1": p1, "p2": p2, "a0": a0, "au": au, "ad": ad, "as": across, "aou": aou, "aod": aod,
        "af": af, "a3": a3, "k": compute, "r0": r0, "rr": rr, "rn": rn, "rt": rt, "rf": rf, "p3": p3, "p4": p4,
        "end": end,
    }
    for name, *args in PLAN:
        steps[name](*args)
    for i, out in enumerate((pk_out, pv_out)):
        copy = pltpu.make_async_copy(pout.at[i], out, load_sem.at[i])
        copy.start()
        stores.append(copy)
    for phase, c in begun:
        all_of(phase, c, dp_send)
    copies.finish()
    for copy in stores:
        copy.wait()


def hand_on(*refs):
    ins, outs, held, sem = refs[:5], refs[5:10], refs[10:15], refs[15]
    loads = [pltpu.make_async_copy(a, b, sem.at[0, i]) for i, (a, b) in enumerate(zip(ins, held))]
    stores = [pltpu.make_async_copy(a, b, sem.at[1, i]) for i, (a, b) in enumerate(zip(held, outs))]
    for copy in loads:
        copy.start()
    for load, copy in zip(loads, stores):
        load.wait()
        copy.start()
    for copy in stores:
        copy.wait()


def on_device(resp_q, resp_k, resp_v, resp_grad, prompt_k, prompt_v, group, resp_len, prompt_used):
    rows, width = resp_q.shape[2:]
    shard = prompt_k.shape[2]
    count = lax.axis_size("dp")
    plen = shard * lax.axis_size("seq")
    heads = width // HEAD // CHUNKS
    wide = pltpu.VMEM((rows, width), BF16)
    prompt = pltpu.VMEM((2, shard, width), BF16)
    pieces = pltpu.VMEM((CHUNKS, count, TILE, HEAD), BF16)
    whole = pltpu.VMEM((CHUNKS, 2, heads, plen, HEAD), BF16)
    shape = lambda r: jax.ShapeDtypeStruct((r, width), BF16)
    hbm = pl.BlockSpec(memory_space=pl.ANY)
    scalar = pl.BlockSpec(memory_space=pltpu.SMEM)
    many = 18 * 2 * CHUNKS
    outs = pl.pallas_call(
        functools.partial(kernel, count, heads),
        in_specs=[hbm] * 6 + [scalar] * 3,
        out_specs=[hbm] * 5,
        out_shape=[shape(rows)] * 3 + [shape(shard)] * 2,
        scratch_shapes=[wide] * 7 + [prompt] * 2 + [pieces] + [whole] * 2 + [
            pltpu.VMEM((CHUNKS, 2, 2, 2, heads // 2, shard, HEAD), BF16),
            pltpu.VMEM((CHUNKS, 2, 2, 2, heads, shard, HEAD), BF16),
            pltpu.VMEM((CHUNKS, 2, heads, NX * shard, HEAD), BF16),
            pltpu.VMEM((CHUNKS, 2, heads, shard, HEAD), BF16),
        ] + [pieces] * 2 + [
            pltpu.VMEM((plen + rows, rows), F32),
            pltpu.SMEM((count,), jnp.int32),
            pltpu.SemaphoreType.DMA((6,)),
            pltpu.SemaphoreType.DMA((CHUNKS, 3)),
            pltpu.SemaphoreType.DMA((4, CHUNKS)),
            pltpu.SemaphoreType.DMA((4, CHUNKS)),
            pltpu.SemaphoreType.DMA((many,)),
            pltpu.SemaphoreType.DMA((many,)),
        ] + [pltpu.VMEM((count, TILE, HEAD), BF16)] * (2 * CHUNKS),
        compiler_params=pltpu.CompilerParams(
            collective_id=0, has_side_effects=True, vmem_limit_bytes=56 * 2**20
        ),
    )(
        resp_q[0, 0], resp_k[0, 0], resp_v[0, 0], resp_grad[0, 0], prompt_k[0, 0], prompt_v[0, 0],
        group, prompt_used, resp_len[0],
    )
    buffers = [pltpu.VMEM(a.shape, BF16) for a in outs]
    outs = pl.pallas_call(
        hand_on,
        in_specs=[hbm] * 5,
        out_specs=[hbm] * 5,
        out_shape=[shape(rows)] * 3 + [shape(shard)] * 2,
        scratch_shapes=buffers + [pltpu.SemaphoreType.DMA((2, 5))],
        compiler_params=pltpu.CompilerParams(vmem_limit_bytes=56 * 2**20),
    )(*outs)
    return tuple(a[None, None] for a in outs)


def solution(mesh):
    split = P("dp", "seq", None, None)
    return jax.shard_map(
        on_device,
        mesh=mesh,
        in_specs=(split,) * 6 + (P(), P("dp", "seq"), P()),
        out_specs=(split,) * 5,
        check_vma=False,
    )
```

```python
import functools

import jax
import jax.numpy as jnp
from jax import lax
from jax.experimental import pallas as pl
from jax.experimental.pallas import tpu as pltpu
from jax.sharding import PartitionSpec as P

HEAD = 128
TILE = 16
CHUNKS = 4
NX = 4
NEG = -1e30
LOG2E = 1.4426950408889634
NT = (((1,), (1,)), ((), ()))
TN = (((0,), (0,)), ((), ()))
NN = (((1,), (0,)), ((), ()))
MESH = pl.DeviceIdType.MESH
BF16 = jnp.bfloat16
F32 = jnp.float32

GATHER_Y_FIRST = ((True, False), (True, False), (True, True), (True, True))
SCATTER_Y_LAST = ((True, False), (True, False), (True, True), (True, True))


PLAN = (
    ("p1", 2), ("p1", 0), ("prep",), ("p2", 2), ("p2", 0), ("p1", 1), ("a0", 2), ("p1", 3), ("a0", 0), ("as", 2, 0),
    ("as", 2, 1), ("au", 2, 0), ("p2", 1), ("ad", 0, 1), ("as", 0, 0), ("au", 0, 1), ("p2", 3), ("aou", 2, 0),
    ("aod", 2, 0), ("aou", 2, 1), ("ad", 2, 1), ("au", 2, 1), ("ad", 2, 0), ("aod", 2, 1), ("a0", 1), ("af", 0, 1),
    ("aod", 0, 0), ("au", 0, 0), ("aou", 0, 0), ("ad", 0, 0), ("a0", 3), ("a3", 2), ("k", 2, 0), ("k", 2, 1),
    ("k", 2, 2), ("as", 1, 0), ("au", 1, 1), ("ad", 1, 1), ("ad", 1, 0), ("a3", 0), ("k", 2, 3), ("r0", 2, 0),
    ("au", 1, 0), ("r0", 2, 1), ("k", 0, 0), ("k", 0, 1), ("k", 0, 2), ("af", 1, 1), ("aou", 1, 0), ("aod", 1, 0),
    ("as", 3, 1), ("k", 0, 3), ("r0", 0, 1), ("as", 3, 0), ("rn", 2, 0, 1, 1), ("rn", 2, 0, 1, 0), ("r0", 0, 0),
    ("rn", 2, 1, 1, 1), ("rn", 2, 1, 1, 0), ("a3", 1), ("k", 1, 0), ("k", 1, 1), ("k", 1, 2), ("au", 3, 0),
    ("aou", 3, 0), ("aou", 3, 1), ("aod", 3, 1), ("au", 3, 1), ("aod", 3, 0), ("ad", 3, 0), ("rt", 2, 0),
    ("ad", 3, 1), ("k", 1, 3), ("r0", 1, 1), ("rn", 2, 1, 0, 1), ("rn", 0, 0, 1, 0), ("rn", 2, 1, 0, 0),
    ("rr", 0, 1), ("rn", 2, 0, 0, 0), ("rn", 0, 0, 1, 1), ("rt", 2, 1), ("rn", 2, 0, 0, 1), ("rn", 0, 0, 0, 0),
    ("rn", 0, 0, 0, 1), ("a3", 3), ("k", 3, 0), ("k", 3, 1), ("k", 3, 2), ("k", 3, 3), ("r0", 3, 0), ("rt", 0, 0),
    ("rn", 0, 1, 0, 1), ("rn", 0, 1, 0, 0), ("rf", 2, 0), ("r0", 3, 1), ("rf", 2, 1), ("p3", 2), ("rn", 3, 0, 1, 1),
    ("rn", 3, 0, 1, 0), ("r0", 1, 0), ("rf", 0, 0), ("rf", 0, 1), ("p3", 0), ("rn", 3, 1, 1, 0), ("rn", 3, 1, 1, 1),
    ("rr", 1, 1), ("rt", 3, 0), ("rn", 1, 0, 1, 1), ("rn", 1, 0, 1, 0), ("rn", 3, 0, 0, 1), ("p4", 2),
    ("rn", 3, 0, 0, 0), ("rn", 3, 1, 0, 1), ("rt", 3, 1), ("rn", 1, 0, 0, 1), ("rn", 3, 1, 0, 0), ("p4", 0),
    ("rn", 1, 0, 0, 0), ("rt", 1, 0), ("rn", 1, 1, 0, 0), ("rf", 3, 0), ("rn", 1, 1, 0, 1), ("rf", 3, 1), ("p3", 3),
    ("rf", 1, 0), ("rf", 1, 1), ("p3", 1), ("end", 0), ("p4", 3), ("end", 2), ("p4", 1), ("end", 3), ("end", 1),
)


def dot(a, b, dims):
    return lax.dot_general(a, b, dims, preferred_element_type=F32)


def head_grads(q, g, kp, ko, vp, vo, bias_p, bias_o, scale):
    c = scale * LOG2E
    sp = dot(kp, q, NT) * c + bias_p
    so = dot(ko, q, NT) * c + bias_o
    top = jnp.maximum(jnp.max(sp, 0, keepdims=True), jnp.max(so, 0, keepdims=True))
    pp = jnp.exp2(sp - top)
    po = jnp.exp2(so - top)
    inv = 1.0 / (jnp.sum(pp, 0, keepdims=True) + jnp.sum(po, 0, keepdims=True))
    dp = dot(vp, g, NT)
    do = dot(vo, g, NT)
    delta = (jnp.sum(pp * dp, 0, keepdims=True) + jnp.sum(po * do, 0, keepdims=True)) * inv
    pp = pp * inv
    po = po * inv
    lp = pp.astype(BF16)
    lo = po.astype(BF16)
    tp = (pp * (dp - delta)).astype(BF16)
    to = (po * (do - delta)).astype(BF16)
    gq = (dot(tp, kp, TN) + dot(to, ko, TN)) * scale
    gko = dot(to, q, NN) * scale
    gvo = dot(lo, g, NN)
    gkp = dot(tp, q, NN) * scale
    gvp = dot(lp, g, NN)
    return tuple(x.astype(BF16) for x in (gq, gko, gvo, gkp, gvp))


class Copies:
    def __init__(self, send, recv):
        self.send, self.recv, self.held = send, recv, {}

    def start(self, name, src, dst, target):
        i = len(self.held)
        copy = pltpu.make_async_remote_copy(
            src_ref=src, dst_ref=dst, send_sem=self.send.at[i], recv_sem=self.recv.at[i],
            device_id=target, device_id_type=MESH,
        )
        copy.start()
        self.held[name] = copy

    def arrived(self, name):
        self.held[name].wait_recv()

    def finish(self):
        for copy in self.held.values():
            copy.wait_send()


def kernel(
    count, heads,
    q_in, k_in, v_in, g_in, pk_in, pv_in, group, used_in, len_in,
    gq, gk, gv, pout,
    q, k, v, g, pin, chosen, gat, part, half_in, full_in, row_in, side_in,
    fin, ordered, bias, inverse,
    load_sem, dp_send, dp_recv, seq_send, seq_recv, *held,
):
    stage, back = held[:CHUNKS], held[CHUNKS:]
    rows = q.shape[0]
    shard = pin.shape[1]
    plen = gat.shape[3]
    scale = HEAD**-0.5
    blocks = shard // TILE
    dp = lax.axis_index("dp")
    seq = lax.axis_index("seq")
    yh, x = seq // NX, seq % NX
    x_up, x_down, x_far = (x + 1) % NX, (x + NX - 1) % NX, (x + 2) % NX
    up = (dp, yh * NX + x_up)
    down = (dp, yh * NX + x_down)
    side = (dp, (1 - yh) * NX + x)
    copies = Copies(seq_send, seq_recv)

    def shard_rows(y, xx):
        return pl.ds(pl.multiple_of((y * NX + xx) * shard, shard), shard)

    def place(j):
        h = lax.rem(lax.div(j, blocks), heads)
        return lax.div(j, heads * blocks), h, pl.multiple_of(lax.rem(j, blocks) * TILE, TILE)

    def in_shard(ref, c, j):
        kv, h, r = place(j)
        cols = pl.multiple_of((c * heads + h) * HEAD, HEAD)
        return ref.at[kv, pl.ds(r, TILE), pl.ds(cols, HEAD)]

    def spread(phase, c, src, dst):
        def one(k, carry):
            step = lax.div(k + 1, 2)
            j = dp + count // 2 + jnp.where(lax.rem(k, 2) == 0, step, -step)
            j = jnp.where(j >= count, j - count, j)
            pltpu.make_async_remote_copy(
                src_ref=src(j), dst_ref=dst, send_sem=dp_send.at[phase, c],
                recv_sem=dp_recv.at[phase, c], device_id=(j, seq), device_id_type=MESH,
            ).start()
            return carry

        begun.append((phase, c))
        lax.fori_loop(0, count - 1, one, 0)

    begun = []

    def all_of(phase, c, sems):
        some = chosen.at[c, pl.ds(0, count - 1)]
        pltpu.make_async_copy(some, some, sems.at[phase, c]).wait()

    mine = place(dp)

    def p1(c):
        spread(0, c, lambda j: in_shard(pin, c, j), stage[c].at[dp])

    def p2(c):
        stage[c][dp] = in_shard(pin, c, dp)[...]
        all_of(0, c, dp_recv)

        def pick(b, carry):
            chosen[c, b] = stage[c][group[b]]
            return carry

        lax.fori_loop(0, count, pick, 0)
        kv, h, r = mine
        dst = gat.at[c, kv, h, pl.ds(pl.multiple_of(seq * shard + r, TILE), TILE)]
        spread(1, c, lambda j: chosen.at[c, j], dst)
        dst[...] = chosen[c, dp]

    def a0(c):
        all_of(1, c, dp_recv)
        for u in (0, 1):
            own = gat.at[c, u, :, shard_rows(yh, x)]
            for name, to in (("side", side), ("up", up), ("down", down)):
                copies.start(("a", c, u, name), own, own, to)

    def relay_up(c, u, name, y):
        piece = gat.at[c, u, pl.ds(0, heads // 2), shard_rows(y, x_down)]
        copies.start(("a", c, u, name), piece, piece, up)

    def relay_down(c, u, name, y):
        piece = gat.at[c, u, pl.ds(heads // 2, heads // 2), shard_rows(y, x_up)]
        copies.start(("a", c, u, name), piece, piece, down)

    def to_side(c, u, name, xx):
        piece = gat.at[c, u, :, shard_rows(yh, xx)]
        copies.start(("a", c, u, name), piece, piece, side)

    def au(c, u):
        copies.arrived(("a", c, u, "up"))
        relay_up(c, u, "up2", yh)
        if not GATHER_Y_FIRST[c][u]:
            to_side(c, u, "sup", x_down)

    def ad(c, u):
        copies.arrived(("a", c, u, "down"))
        relay_down(c, u, "down2", yh)
        if not GATHER_Y_FIRST[c][u]:
            to_side(c, u, "sdn", x_up)

    def across(c, u):
        copies.arrived(("a", c, u, "side"))
        other = gat.at[c, u, :, shard_rows(1 - yh, x)]
        copies.start(("a", c, u, "oup"), other, other, up)
        copies.start(("a", c, u, "odn"), other, other, down)

    def aou(c, u):
        copies.arrived(("a", c, u, "oup"))
        relay_up(c, u, "oup2", 1 - yh)

    def aod(c, u):
        copies.arrived(("a", c, u, "odn"))
        relay_down(c, u, "odn2", 1 - yh)

    def af(c, u):
        copies.arrived(("a", c, u, "up2"))
        copies.arrived(("a", c, u, "down2"))
        to_side(c, u, "sfar", x_far)

    def a3(c):
        for u in (0, 1):
            if GATHER_Y_FIRST[c][u]:
                names = ("up2", "down2", "oup2", "odn2")
            else:
                names = ("side", "sup", "sdn", "sfar")
            for name in names:
                copies.arrived(("a", c, u, name))

    def compute(c, h):
        cols = pl.ds((c * heads + h) * HEAD, HEAD)
        gq[:, cols], gk[:, cols], gv[:, cols], part[c, 0, h], part[c, 1, h] = head_grads(
            q[:, cols], g[:, cols], gat[c, 0, h], k[:, cols], gat[c, 1, h], v[:, cols],
            bias[:plen], bias[plen:], scale,
        )

    def add(dst, src):
        dst[...] = (dst[...].astype(F32) + src[...].astype(F32)).astype(BF16)

    def far_halves(c, u, r, y):
        for d, lo, to in ((0, 0, down), (1, heads // 2, up)):
            copies.start(
                ("r", c, u, r, "half", d),
                part.at[c, u, pl.ds(lo, heads // 2), shard_rows(y, x_far)], half_in.at[c, u, r, d], to,
            )

    def row_of(r):
        return yh if r == 0 else 1 - yh

    def r0(c, u):
        if SCATTER_Y_LAST[c][u]:
            for r in (1, 0):
                far_halves(c, u, r, row_of(r))
        else:
            src = part.at[c, u, :, pl.ds(pl.multiple_of((1 - yh) * NX * shard, shard), NX * shard)]
            copies.start(("r", c, u, "row"), src, row_in.at[c, u], side)

    def rr(c, u):
        copies.arrived(("r", c, u, "row"))
        for xx in (x_far, x_down, x_up, x):
            src = row_in.at[c, u, :, pl.ds(pl.multiple_of(xx * shard, shard), shard)]
            add(part.at[c, u, :, shard_rows(yh, xx)], src)
            if xx is x_far:
                far_halves(c, u, 0, yh)

    def rn(c, u, r, d):
        lo, xx, to = ((0, x_down, down), (heads // 2, x_up, up))[d]
        copies.arrived(("r", c, u, r, "half", d))
        add(part.at[c, u, pl.ds(lo, heads // 2), shard_rows(row_of(r), xx)], half_in.at[c, u, r, d])
        src = part.at[c, u, :, shard_rows(row_of(r), xx)]
        copies.start(("r", c, u, r, "full", d), src, full_in.at[c, u, r, d], to)

    def total(c, u, r):
        for d in (0, 1):
            copies.arrived(("r", c, u, r, "full", d))
        own = part[c, u, :, shard_rows(row_of(r), x)].astype(F32)
        return own + full_in[c, u, r, 0].astype(F32) + full_in[c, u, r, 1].astype(F32)

    def rt(c, u):
        sent = part.at[c, u, :, shard_rows(1 - yh, x)]
        sent[...] = total(c, u, 1).astype(BF16)
        copies.start(("r", c, u, "side"), sent, side_in.at[c, u], side)

    def rf(c, u):
        value = total(c, u, 0)
        if SCATTER_Y_LAST[c][u]:
            copies.arrived(("r", c, u, "side"))
            value = value + side_in[c, u].astype(F32)
        n = heads * blocks
        fin[c, u * n : (u + 1) * n] = value.astype(BF16).reshape(n, TILE, HEAD)

    def p3(c):
        back[c][dp] = fin[c, dp]
        spread(2, c, lambda j: fin.at[c, j], back[c].at[dp])

    def p4(c):
        all_of(2, c, dp_recv)

        def pick(p, carry):
            ordered[c, p] = back[c][inverse[p]]
            return carry

        lax.fori_loop(0, count, pick, 0)
        dst = in_shard(pout, c, dp)
        dst[...] = ordered[c, dp]
        spread(3, c, lambda j: ordered.at[c, j], dst)

    loads = [
        pltpu.make_async_copy(a, b, load_sem.at[i])
        for i, (a, b) in enumerate(
            ((pk_in, pin.at[0]), (pv_in, pin.at[1]), (q_in, q), (k_in, k), (v_in, v), (g_in, g))
        )
    ]
    for copy in loads:
        copy.start()
    barrier = pltpu.get_barrier_semaphore()

    def greet(i, carry):
        pl.semaphore_signal(barrier, inc=1, device_id=((dp + i) % count, seq), device_id_type=MESH)
        return carry

    lax.fori_loop(1, count, greet, 0)
    for target in (up, down, side):
        pl.semaphore_signal(barrier, inc=1, device_id=target, device_id_type=MESH)
    pl.semaphore_wait(barrier, count - 1 + 3)
    loads[0].wait()
    loads[1].wait()

    def prepare():
        length = len_in[0, 0]
        used = used_in[group[dp]]
        bias[:plen] = jnp.where(lax.broadcasted_iota(jnp.int32, (plen, rows), 0) < used, 0.0, NEG)
        key = lax.broadcasted_iota(jnp.int32, (rows, rows), 0)
        query = lax.broadcasted_iota(jnp.int32, (rows, rows), 1)
        bias[plen:] = jnp.where((key <= query) & (key < length), 0.0, NEG)

        def invert(p, carry):
            found = jnp.int32(0)
            for b in range(count):
                found = jnp.where(group[b] == p, b, found)
            inverse[p] = found
            return carry

        lax.fori_loop(0, count, invert, 0)
        for copy in loads[2:]:
            copy.wait()
        for i in range(0, g.shape[1], 512):
            live = lax.broadcasted_iota(jnp.int32, (rows, 512), 0) < length
            g[:, i : i + 512] = jnp.where(live, g[:, i : i + 512], jnp.zeros((rows, 512), BF16))

    def end(c):
        all_of(3, c, dp_recv)

    steps = {
        "prep": prepare, "p1": p1, "p2": p2, "a0": a0, "au": au, "ad": ad, "as": across, "aou": aou, "aod": aod,
        "af": af, "a3": a3, "k": compute, "r0": r0, "rr": rr, "rn": rn, "rt": rt, "rf": rf, "p3": p3, "p4": p4,
        "end": end,
    }
    for name, *args in PLAN:
        steps[name](*args)
    for phase, c in begun:
        all_of(phase, c, dp_send)
    copies.finish()


def hand_on(gq, gk, gv, gp, *refs):
    outs, sem = refs[:5], refs[5]
    ins = (gq, gk, gv, gp.at[0], gp.at[1])
    copies = [pltpu.make_async_copy(a, b, sem.at[i]) for i, (a, b) in enumerate(zip(ins, outs))]
    for copy in copies:
        copy.start()
    for copy in copies:
        copy.wait()


def on_device(resp_q, resp_k, resp_v, resp_grad, prompt_k, prompt_v, group, resp_len, prompt_used):
    rows, width = resp_q.shape[2:]
    shard = prompt_k.shape[2]
    count = lax.axis_size("dp")
    plen = shard * lax.axis_size("seq")
    heads = width // HEAD // CHUNKS
    wide = pltpu.VMEM((rows, width), BF16)
    prompt = pltpu.VMEM((2, shard, width), BF16)
    pieces = pltpu.VMEM((CHUNKS, count, TILE, HEAD), BF16)
    whole = pltpu.VMEM((CHUNKS, 2, heads, plen, HEAD), BF16)
    shape = lambda r: jax.ShapeDtypeStruct((r, width), BF16)
    hbm = pl.BlockSpec(memory_space=pl.ANY)
    vmem = pl.BlockSpec(memory_space=pltpu.VMEM)
    scalar = pl.BlockSpec(memory_space=pltpu.SMEM)
    many = 18 * 2 * CHUNKS
    outs = pl.pallas_call(
        functools.partial(kernel, count, heads),
        in_specs=[hbm] * 6 + [scalar] * 3,
        out_specs=[vmem] * 4,
        out_shape=[wide] * 3 + [prompt],
        scratch_shapes=[wide] * 4 + [prompt] + [pieces] + [whole] * 2 + [
            pltpu.VMEM((CHUNKS, 2, 2, 2, heads // 2, shard, HEAD), BF16),
            pltpu.VMEM((CHUNKS, 2, 2, 2, heads, shard, HEAD), BF16),
            pltpu.VMEM((CHUNKS, 2, heads, NX * shard, HEAD), BF16),
            pltpu.VMEM((CHUNKS, 2, heads, shard, HEAD), BF16),
        ] + [pieces] * 2 + [
            pltpu.VMEM((plen + rows, rows), F32),
            pltpu.SMEM((count,), jnp.int32),
            pltpu.SemaphoreType.DMA((6,)),
            pltpu.SemaphoreType.DMA((4, CHUNKS)),
            pltpu.SemaphoreType.DMA((4, CHUNKS)),
            pltpu.SemaphoreType.DMA((many,)),
            pltpu.SemaphoreType.DMA((many,)),
        ] + [pltpu.VMEM((count, TILE, HEAD), BF16)] * (2 * CHUNKS),
        compiler_params=pltpu.CompilerParams(
            collective_id=0, has_side_effects=True, vmem_limit_bytes=58 * 2**20
        ),
    )(
        resp_q[0, 0], resp_k[0, 0], resp_v[0, 0], resp_grad[0, 0], prompt_k[0, 0], prompt_v[0, 0],
        group, prompt_used, resp_len,
    )
    outs = pl.pallas_call(
        hand_on,
        in_specs=[vmem] * 4,
        out_specs=[hbm] * 5,
        out_shape=[shape(rows)] * 3 + [shape(shard)] * 2,
        scratch_shapes=[pltpu.SemaphoreType.DMA((5,))],
        compiler_params=pltpu.CompilerParams(vmem_limit_bytes=16 * 2**20),
    )(*outs)
    return tuple(a[None, None] for a in outs)


def solution(mesh):
    split = P("dp", "seq", None, None)
    return jax.shard_map(
        on_device,
        mesh=mesh,
        in_specs=(split,) * 6 + (P(), P("dp", "seq"), P()),
        out_specs=(split,) * 5,
        check_vma=False,
    )
```

```python
import functools

import jax
import jax.numpy as jnp
from jax import lax
from jax.experimental import pallas as pl
from jax.experimental.pallas import tpu as pltpu
from jax.sharding import PartitionSpec as P

HEAD = 128
TILE = 16
CHUNKS = 4
NX = 4
NEG = -1e30
LOG2E = 1.4426950408889634
NT = (((1,), (1,)), ((), ()))
TN = (((0,), (0,)), ((), ()))
NN = (((1,), (0,)), ((), ()))
MESH = pl.DeviceIdType.MESH
BF16 = jnp.bfloat16
F32 = jnp.float32

GATHER_Y_FIRST = ((True, False), (True, False), (True, True), (True, True))
SCATTER_Y_LAST = ((True, False), (True, False), (True, True), (True, True))


PLAN = (
    ("p1", 2), ("p1", 0), ("prep",), ("p2", 2), ("p2", 0), ("p1", 1), ("a0", 2), ("p1", 3), ("a0", 0), ("as", 2, 0),
    ("as", 2, 1), ("au", 2, 0), ("p2", 1), ("ad", 0, 1), ("as", 0, 0), ("au", 0, 1), ("p2", 3), ("aou", 2, 0),
    ("aod", 2, 0), ("aou", 2, 1), ("ad", 2, 1), ("au", 2, 1), ("ad", 2, 0), ("aod", 2, 1), ("a0", 1), ("af", 0, 1),
    ("aod", 0, 0), ("au", 0, 0), ("aou", 0, 0), ("ad", 0, 0), ("a0", 3), ("a3", 2), ("k", 2, 0), ("k", 2, 1),
    ("k", 2, 2), ("as", 1, 0), ("au", 1, 1), ("ad", 1, 1), ("ad", 1, 0), ("a3", 0), ("k", 2, 3), ("r0", 2, 0),
    ("au", 1, 0), ("r0", 2, 1), ("k", 0, 0), ("k", 0, 1), ("k", 0, 2), ("af", 1, 1), ("aou", 1, 0), ("aod", 1, 0),
    ("as", 3, 1), ("k", 0, 3), ("r0", 0, 1), ("as", 3, 0), ("rn", 2, 0, 1, 1), ("rn", 2, 0, 1, 0), ("r0", 0, 0),
    ("rn", 2, 1, 1, 1), ("rn", 2, 1, 1, 0), ("a3", 1), ("k", 1, 0), ("k", 1, 1), ("k", 1, 2), ("au", 3, 0),
    ("aou", 3, 0), ("aou", 3, 1), ("aod", 3, 1), ("au", 3, 1), ("aod", 3, 0), ("ad", 3, 0), ("rt", 2, 0),
    ("ad", 3, 1), ("k", 1, 3), ("r0", 1, 1), ("rn", 2, 1, 0, 1), ("rn", 0, 0, 1, 0), ("rn", 2, 1, 0, 0),
    ("rr", 0, 1), ("rn", 2, 0, 0, 0), ("rn", 0, 0, 1, 1), ("rt", 2, 1), ("rn", 2, 0, 0, 1), ("rn", 0, 0, 0, 0),
    ("rn", 0, 0, 0, 1), ("a3", 3), ("k", 3, 0), ("k", 3, 1), ("k", 3, 2), ("k", 3, 3), ("r0", 3, 0), ("rt", 0, 0),
    ("rn", 0, 1, 0, 1), ("rn", 0, 1, 0, 0), ("rf", 2, 0), ("r0", 3, 1), ("rf", 2, 1), ("p3", 2), ("rn", 3, 0, 1, 1),
    ("rn", 3, 0, 1, 0), ("r0", 1, 0), ("rf", 0, 0), ("rf", 0, 1), ("p3", 0), ("rn", 3, 1, 1, 0), ("rn", 3, 1, 1, 1),
    ("rr", 1, 1), ("rt", 3, 0), ("rn", 1, 0, 1, 1), ("rn", 1, 0, 1, 0), ("rn", 3, 0, 0, 1), ("p4", 2),
    ("rn", 3, 0, 0, 0), ("rn", 3, 1, 0, 1), ("rt", 3, 1), ("rn", 1, 0, 0, 1), ("rn", 3, 1, 0, 0), ("p4", 0),
    ("rn", 1, 0, 0, 0), ("rt", 1, 0), ("rn", 1, 1, 0, 0), ("rf", 3, 0), ("rn", 1, 1, 0, 1), ("rf", 3, 1), ("p3", 3),
    ("rf", 1, 0), ("rf", 1, 1), ("p3", 1), ("end", 0), ("p4", 3), ("end", 2), ("p4", 1), ("flush", 2), ("end", 3),
    ("end", 1),
)


def dot(a, b, dims):
    return lax.dot_general(a, b, dims, preferred_element_type=F32)


def head_grads(q, g, kp, ko, vp, vo, bias_p, bias_o, scale):
    c = scale * LOG2E
    sp = dot(kp, q, NT) * c + bias_p
    so = dot(ko, q, NT) * c + bias_o
    top = jnp.maximum(jnp.max(sp, 0, keepdims=True), jnp.max(so, 0, keepdims=True))
    pp = jnp.exp2(sp - top)
    po = jnp.exp2(so - top)
    inv = 1.0 / (jnp.sum(pp, 0, keepdims=True) + jnp.sum(po, 0, keepdims=True))
    dp = dot(vp, g, NT)
    do = dot(vo, g, NT)
    delta = (jnp.sum(pp * dp, 0, keepdims=True) + jnp.sum(po * do, 0, keepdims=True)) * inv
    pp = pp * inv
    po = po * inv
    lp = pp.astype(BF16)
    lo = po.astype(BF16)
    tp = (pp * (dp - delta)).astype(BF16)
    to = (po * (do - delta)).astype(BF16)
    gq = (dot(tp, kp, TN) + dot(to, ko, TN)) * scale
    gko = dot(to, q, NN) * scale
    gvo = dot(lo, g, NN)
    gkp = dot(tp, q, NN) * scale
    gvp = dot(lp, g, NN)
    return tuple(x.astype(BF16) for x in (gq, gko, gvo, gkp, gvp))


class Copies:
    def __init__(self, send, recv):
        self.send, self.recv, self.held, self.ended = send, recv, {}, set()

    def start(self, name, src, dst, target):
        i = len(self.held)
        copy = pltpu.make_async_remote_copy(
            src_ref=src, dst_ref=dst, send_sem=self.send.at[i], recv_sem=self.recv.at[i],
            device_id=target, device_id_type=MESH,
        )
        copy.start()
        self.held[name] = copy

    def arrived(self, name):
        self.held[name].wait_recv()

    def finish(self):
        for name in [name for name in self.held if name not in self.ended]:
            self.held[name].wait_send()
            self.ended.add(name)


def kernel(
    count, heads,
    q_in, k_in, v_in, g_in, pk_in, pv_in, group, used_in, len_in,
    gq, gk, gv, pout,
    q, k, v, g, pin, chosen, gat, part, half_in, full_in, row_in, side_in,
    fin, ordered, bias, inverse,
    load_sem, dp_send, dp_recv, seq_send, seq_recv, *held,
):
    stage, back = held[:CHUNKS], held[CHUNKS:]
    rows = q.shape[0]
    shard = pin.shape[1]
    plen = gat.shape[3]
    scale = HEAD**-0.5
    blocks = shard // TILE
    dp = lax.axis_index("dp")
    seq = lax.axis_index("seq")
    yh, x = seq // NX, seq % NX
    x_up, x_down, x_far = (x + 1) % NX, (x + NX - 1) % NX, (x + 2) % NX
    up = (dp, yh * NX + x_up)
    down = (dp, yh * NX + x_down)
    side = (dp, (1 - yh) * NX + x)
    copies = Copies(seq_send, seq_recv)

    def shard_rows(y, xx):
        return pl.ds(pl.multiple_of((y * NX + xx) * shard, shard), shard)

    def place(j):
        h = lax.rem(lax.div(j, blocks), heads)
        return lax.div(j, heads * blocks), h, pl.multiple_of(lax.rem(j, blocks) * TILE, TILE)

    def in_shard(ref, c, j):
        kv, h, r = place(j)
        cols = pl.multiple_of((c * heads + h) * HEAD, HEAD)
        return ref.at[kv, pl.ds(r, TILE), pl.ds(cols, HEAD)]

    def spread(phase, c, src, dst):
        def one(k, carry):
            step = lax.div(k + 1, 2)
            j = dp + count // 2 + jnp.where(lax.rem(k, 2) == 0, step, -step)
            j = jnp.where(j >= count, j - count, j)
            pltpu.make_async_remote_copy(
                src_ref=src(j), dst_ref=dst, send_sem=dp_send.at[phase, c],
                recv_sem=dp_recv.at[phase, c], device_id=(j, seq), device_id_type=MESH,
            ).start()
            return carry

        begun.append((phase, c))
        lax.fori_loop(0, count - 1, one, 0)

    begun = []

    def all_of(phase, c, sems):
        some = chosen.at[c, pl.ds(0, count - 1)]
        pltpu.make_async_copy(some, some, sems.at[phase, c]).wait()

    mine = place(dp)

    def p1(c):
        spread(0, c, lambda j: in_shard(pin, c, j), stage[c].at[dp])

    def p2(c):
        stage[c][dp] = in_shard(pin, c, dp)[...]
        all_of(0, c, dp_recv)

        def pick(b, carry):
            chosen[c, b] = stage[c][group[b]]
            return carry

        lax.fori_loop(0, count, pick, 0)
        kv, h, r = mine
        dst = gat.at[c, kv, h, pl.ds(pl.multiple_of(seq * shard + r, TILE), TILE)]
        spread(1, c, lambda j: chosen.at[c, j], dst)
        dst[...] = chosen[c, dp]

    def a0(c):
        all_of(1, c, dp_recv)
        for u in (0, 1):
            own = gat.at[c, u, :, shard_rows(yh, x)]
            for name, to in (("side", side), ("up", up), ("down", down)):
                copies.start(("a", c, u, name), own, own, to)

    def relay_up(c, u, name, y):
        piece = gat.at[c, u, pl.ds(0, heads // 2), shard_rows(y, x_down)]
        copies.start(("a", c, u, name), piece, piece, up)

    def relay_down(c, u, name, y):
        piece = gat.at[c, u, pl.ds(heads // 2, heads // 2), shard_rows(y, x_up)]
        copies.start(("a", c, u, name), piece, piece, down)

    def to_side(c, u, name, xx):
        piece = gat.at[c, u, :, shard_rows(yh, xx)]
        copies.start(("a", c, u, name), piece, piece, side)

    def au(c, u):
        copies.arrived(("a", c, u, "up"))
        relay_up(c, u, "up2", yh)
        if not GATHER_Y_FIRST[c][u]:
            to_side(c, u, "sup", x_down)

    def ad(c, u):
        copies.arrived(("a", c, u, "down"))
        relay_down(c, u, "down2", yh)
        if not GATHER_Y_FIRST[c][u]:
            to_side(c, u, "sdn", x_up)

    def across(c, u):
        copies.arrived(("a", c, u, "side"))
        other = gat.at[c, u, :, shard_rows(1 - yh, x)]
        copies.start(("a", c, u, "oup"), other, other, up)
        copies.start(("a", c, u, "odn"), other, other, down)

    def aou(c, u):
        copies.arrived(("a", c, u, "oup"))
        relay_up(c, u, "oup2", 1 - yh)

    def aod(c, u):
        copies.arrived(("a", c, u, "odn"))
        relay_down(c, u, "odn2", 1 - yh)

    def af(c, u):
        copies.arrived(("a", c, u, "up2"))
        copies.arrived(("a", c, u, "down2"))
        to_side(c, u, "sfar", x_far)

    def a3(c):
        for u in (0, 1):
            if GATHER_Y_FIRST[c][u]:
                names = ("up2", "down2", "oup2", "odn2")
            else:
                names = ("side", "sup", "sdn", "sfar")
            for name in names:
                copies.arrived(("a", c, u, name))

    def compute(c, h):
        cols = pl.ds((c * heads + h) * HEAD, HEAD)
        gq[:, cols], gk[:, cols], gv[:, cols], part[c, 0, h], part[c, 1, h] = head_grads(
            q[:, cols], g[:, cols], gat[c, 0, h], k[:, cols], gat[c, 1, h], v[:, cols],
            bias[:plen], bias[plen:], scale,
        )

    def add(dst, src):
        dst[...] = (dst[...].astype(F32) + src[...].astype(F32)).astype(BF16)

    def far_halves(c, u, r, y):
        for d, lo, to in ((0, 0, down), (1, heads // 2, up)):
            copies.start(
                ("r", c, u, r, "half", d),
                part.at[c, u, pl.ds(lo, heads // 2), shard_rows(y, x_far)], half_in.at[c, u, r, d], to,
            )

    def row_of(r):
        return yh if r == 0 else 1 - yh

    def r0(c, u):
        if SCATTER_Y_LAST[c][u]:
            for r in (1, 0):
                far_halves(c, u, r, row_of(r))
        else:
            src = part.at[c, u, :, pl.ds(pl.multiple_of((1 - yh) * NX * shard, shard), NX * shard)]
            copies.start(("r", c, u, "row"), src, row_in.at[c, u], side)

    def rr(c, u):
        copies.arrived(("r", c, u, "row"))
        for xx in (x_far, x_down, x_up, x):
            src = row_in.at[c, u, :, pl.ds(pl.multiple_of(xx * shard, shard), shard)]
            add(part.at[c, u, :, shard_rows(yh, xx)], src)
            if xx is x_far:
                far_halves(c, u, 0, yh)

    def rn(c, u, r, d):
        lo, xx, to = ((0, x_down, down), (heads // 2, x_up, up))[d]
        copies.arrived(("r", c, u, r, "half", d))
        add(part.at[c, u, pl.ds(lo, heads // 2), shard_rows(row_of(r), xx)], half_in.at[c, u, r, d])
        src = part.at[c, u, :, shard_rows(row_of(r), xx)]
        copies.start(("r", c, u, r, "full", d), src, full_in.at[c, u, r, d], to)

    def total(c, u, r):
        for d in (0, 1):
            copies.arrived(("r", c, u, r, "full", d))
        own = part[c, u, :, shard_rows(row_of(r), x)].astype(F32)
        return own + full_in[c, u, r, 0].astype(F32) + full_in[c, u, r, 1].astype(F32)

    def rt(c, u):
        sent = part.at[c, u, :, shard_rows(1 - yh, x)]
        sent[...] = total(c, u, 1).astype(BF16)
        copies.start(("r", c, u, "side"), sent, side_in.at[c, u], side)

    def rf(c, u):
        value = total(c, u, 0)
        if SCATTER_Y_LAST[c][u]:
            copies.arrived(("r", c, u, "side"))
            value = value + side_in[c, u].astype(F32)
        n = heads * blocks
        fin[c, u * n : (u + 1) * n] = value.astype(BF16).reshape(n, TILE, HEAD)

    def p3(c):
        back[c][dp] = fin[c, dp]
        spread(2, c, lambda j: fin.at[c, j], back[c].at[dp])

    def p4(c):
        all_of(2, c, dp_recv)

        def pick(p, carry):
            ordered[c, p] = back[c][inverse[p]]
            return carry

        lax.fori_loop(0, count, pick, 0)
        dst = in_shard(pout, c, dp)
        dst[...] = ordered[c, dp]
        spread(3, c, lambda j: ordered.at[c, j], dst)

    loads = [
        pltpu.make_async_copy(a, b, load_sem.at[i])
        for i, (a, b) in enumerate(
            ((pk_in, pin.at[0]), (pv_in, pin.at[1]), (q_in, q), (k_in, k), (v_in, v), (g_in, g))
        )
    ]
    for copy in loads:
        copy.start()
    barrier = pltpu.get_barrier_semaphore()

    def greet(i, carry):
        pl.semaphore_signal(barrier, inc=1, device_id=((dp + i) % count, seq), device_id_type=MESH)
        return carry

    lax.fori_loop(1, count, greet, 0)
    for target in (up, down, side):
        pl.semaphore_signal(barrier, inc=1, device_id=target, device_id_type=MESH)
    pl.semaphore_wait(barrier, count - 1 + 3)
    loads[0].wait()
    loads[1].wait()

    def prepare():
        length = len_in[0, 0]
        used = used_in[group[dp]]
        bias[:plen] = jnp.where(lax.broadcasted_iota(jnp.int32, (plen, rows), 0) < used, 0.0, NEG)
        key = lax.broadcasted_iota(jnp.int32, (rows, rows), 0)
        query = lax.broadcasted_iota(jnp.int32, (rows, rows), 1)
        bias[plen:] = jnp.where((key <= query) & (key < length), 0.0, NEG)

        def invert(p, carry):
            found = jnp.int32(0)
            for b in range(count):
                found = jnp.where(group[b] == p, b, found)
            inverse[p] = found
            return carry

        lax.fori_loop(0, count, invert, 0)
        for copy in loads[2:]:
            copy.wait()
        for i in range(0, g.shape[1], 512):
            live = lax.broadcasted_iota(jnp.int32, (rows, 512), 0) < length
            g[:, i : i + 512] = jnp.where(live, g[:, i : i + 512], jnp.zeros((rows, 512), BF16))

    def end(c):
        all_of(3, c, dp_recv)

    def flush(keep):
        copies.finish()
        for phase, c in begun[: len(begun) - keep]:
            all_of(phase, c, dp_send)
        del begun[: len(begun) - keep]

    steps = {
        "prep": prepare, "p1": p1, "p2": p2, "a0": a0, "au": au, "ad": ad, "as": across, "aou": aou, "aod": aod,
        "af": af, "a3": a3, "k": compute, "r0": r0, "rr": rr, "rn": rn, "rt": rt, "rf": rf, "p3": p3, "p4": p4,
        "end": end, "flush": flush,
    }
    for name, *args in PLAN:
        steps[name](*args)
    flush(0)


def hand_on(gq, gk, gv, gp, *refs):
    outs, sem = refs[:5], refs[5]
    ins = (gq, gk, gv, gp.at[0], gp.at[1])
    copies = [pltpu.make_async_copy(a, b, sem.at[i]) for i, (a, b) in enumerate(zip(ins, outs))]
    for copy in copies:
        copy.start()
    for copy in copies:
        copy.wait()


def on_device(resp_q, resp_k, resp_v, resp_grad, prompt_k, prompt_v, group, resp_len, prompt_used):
    rows, width = resp_q.shape[2:]
    shard = prompt_k.shape[2]
    count = lax.axis_size("dp")
    plen = shard * lax.axis_size("seq")
    heads = width // HEAD // CHUNKS
    wide = pltpu.VMEM((rows, width), BF16)
    prompt = pltpu.VMEM((2, shard, width), BF16)
    pieces = pltpu.VMEM((CHUNKS, count, TILE, HEAD), BF16)
    whole = pltpu.VMEM((CHUNKS, 2, heads, plen, HEAD), BF16)
    shape = lambda r: jax.ShapeDtypeStruct((r, width), BF16)
    hbm = pl.BlockSpec(memory_space=pl.ANY)
    vmem = pl.BlockSpec(memory_space=pltpu.VMEM)
    scalar = pl.BlockSpec(memory_space=pltpu.SMEM)
    many = 18 * 2 * CHUNKS
    outs = pl.pallas_call(
        functools.partial(kernel, count, heads),
        in_specs=[hbm] * 6 + [scalar] * 3,
        out_specs=[vmem] * 4,
        out_shape=[wide] * 3 + [prompt],
        scratch_shapes=[wide] * 4 + [prompt] + [pieces] + [whole] * 2 + [
            pltpu.VMEM((CHUNKS, 2, 2, 2, heads // 2, shard, HEAD), BF16),
            pltpu.VMEM((CHUNKS, 2, 2, 2, heads, shard, HEAD), BF16),
            pltpu.VMEM((CHUNKS, 2, heads, NX * shard, HEAD), BF16),
            pltpu.VMEM((CHUNKS, 2, heads, shard, HEAD), BF16),
        ] + [pieces] * 2 + [
            pltpu.VMEM((plen + rows, rows), F32),
            pltpu.SMEM((count,), jnp.int32),
            pltpu.SemaphoreType.DMA((6,)),
            pltpu.SemaphoreType.DMA((4, CHUNKS)),
            pltpu.SemaphoreType.DMA((4, CHUNKS)),
            pltpu.SemaphoreType.DMA((many,)),
            pltpu.SemaphoreType.DMA((many,)),
        ] + [pltpu.VMEM((count, TILE, HEAD), BF16)] * (2 * CHUNKS),
        compiler_params=pltpu.CompilerParams(
            collective_id=0, has_side_effects=True, vmem_limit_bytes=58 * 2**20
        ),
    )(
        resp_q[0, 0], resp_k[0, 0], resp_v[0, 0], resp_grad[0, 0], prompt_k[0, 0], prompt_v[0, 0],
        group, prompt_used, resp_len,
    )
    outs = pl.pallas_call(
        hand_on,
        in_specs=[vmem] * 4,
        out_specs=[hbm] * 5,
        out_shape=[shape(rows)] * 3 + [shape(shard)] * 2,
        scratch_shapes=[pltpu.SemaphoreType.DMA((5,))],
        compiler_params=pltpu.CompilerParams(vmem_limit_bytes=16 * 2**20),
    )(*outs)
    return tuple(a[None, None] for a in outs)


def solution(mesh):
    split = P("dp", "seq", None, None)
    return jax.shard_map(
        on_device,
        mesh=mesh,
        in_specs=(split,) * 6 + (P(), P("dp", "seq"), P()),
        out_specs=(split,) * 5,
        check_vma=False,
    )
```
